32 devices in a mesh: groups: 2 (over y), orient: 4 (over z), cls: 2 (over x), dom: 2 (over core).
Axes of the slice: x: 2, y: 2, z: 4, core: 2. Of those that a mesh axis runs over, the one named last changes fastest.
Arguments:
- particles: bfloat16 [256, 2, 16512], P(('groups', 'orient', 'cls', 'dom')), parts along dimension 0, may hold values from -10 to 10
- ctf_index: int32 [256], P(('groups', 'orient', 'cls', 'dom')), parts along dimension 0, may hold values from 0 to 15
- beta: bfloat16 [256], P(('groups', 'orient', 'cls', 'dom')), parts along dimension 0, may hold values from 10 to 60
- significant: int32 [128, 1], P(('groups', 'orient', 'cls', 'dom')), parts along dimension 0, may hold values from 0 to 3; in each aligned block of 4 rows (0 to 3, 4 to 7, ...) at most 2 rows name the same one
- ctf_table: bfloat16 [16, 16512], replicated, may hold values from 0.049804688 to 1
- references: bfloat16 [4, 4, 4, 2, 16512], P(('groups', 'cls'), 'orient'), parts along dimension 0, may hold values from -4 to 4
- offsets: int32 [10, 2], P('groups'), parts along dimension 0, may hold values from -3 to 3, as said below
Outputs:
- class_post: float32 [256, 2], P(('groups', 'orient', 'cls', 'dom')), parts along dimension 0
- log_evidence: float32 [256], P(('groups', 'orient', 'cls', 'dom')), parts along dimension 0
The draws below stay inside these ranges and needn't reach their ends.
There are 2 independent parts, one for each index of `groups`. The reference program is written for one: setup_inputs(seed, part) draws one part's arguments, and reference() takes and returns one part's arrays. A program takes and returns all parts, laid end to end along the dimension named above; an argument that names none is the same for every part. Nothing has to cross between parts.
Inputs may be any that keep to these rules, and one draw needn't show every extreme that they name: `significant`: each block of 2 particles names 1 different orientation groups; the 4 blocks of one device name any one group at most 2 times. The 5 offsets are distinct pairs.
All inputs are finite; a program needn't handle non-finite values.
Results may differ from the reference program's by a relative error of at most 0.0003.
Values may be sent and summed in bfloat16 or wider, within the bound.
A program may use at most 128 MiB of HBM per device.

```python
import math
import jax
import jax.numpy as jnp
import numpy as np
from jax import lax

BOX = 256
KX = 129
KY = 128
NPIX = 16512
NGRP = 4
OR_G = 4
NCLS = 2
T_OFF = 5
RADIUS = 3
NCTF = 16
BLK = 2
NB = 4
SIG = 1
CAP = 2
PTOT = 128
NBLK = 64


def model_references(key):
    ref_key = jax.random.fold_in(key, 101)
    sorted_key_values = jax.random.fold_in(ref_key, 0)
    ref_shape = (NCLS, NGRP, OR_G, 2, NPIX)
    values = jax.random.normal(sorted_key_values, ref_shape, jnp.float32)
    return jnp.clip(values, -4.0, 4.0)


def model_offsets(key):
    side_count = 2 * RADIUS + 1
    picked = jax.random.permutation(jax.random.fold_in(key, 202), side_count * side_count)[:T_OFF].astype(jnp.int32)
    return jnp.stack([picked % side_count - RADIUS, picked // side_count - RADIUS], axis=1)


def draw_references(key, part):
    return model_references(key).astype(jnp.bfloat16)


def draw_offsets(key, part):
    return model_offsets(key)


def draw_particles(key, part):
    model_refs = model_references(key)
    shifts = model_offsets(key)
    pick_keys = jax.random.split(jax.random.fold_in(key, 303), 5)
    class_pick = jax.random.randint(pick_keys[0], (PTOT,), 0, NCLS)
    group_pick = jax.random.randint(pick_keys[1], (PTOT,), 0, NGRP)
    orient_pick = jax.random.randint(pick_keys[2], (PTOT,), 0, OR_G)
    shift_pick = jax.random.randint(pick_keys[3], (PTOT,), 0, T_OFF)
    chosen = model_refs[class_pick, group_pick, orient_pick]
    true_shift = shifts[shift_pick]
    pixel_index = jnp.arange(NPIX, dtype=jnp.int32)
    freq_x = pixel_index % KX
    freq_y = pixel_index // KX - KY // 2
    phase_rotations = jnp.mod(true_shift[:, 0:1] * freq_x[None, :] + true_shift[:, 1:2] * freq_y[None, :], BOX)
    angles = phase_rotations.astype(jnp.float32) * (2.0 * math.pi / BOX)
    cosines = jnp.cos(angles)
    sines = jnp.sin(angles)
    real_part = chosen[:, 0] * cosines + chosen[:, 1] * sines
    imag_part = chosen[:, 1] * cosines - chosen[:, 0] * sines
    signal = jnp.stack([real_part, imag_part], axis=1)
    noise_part = jnp.clip(jax.random.normal(pick_keys[4], (PTOT, 2, NPIX), jnp.float32), -4.0, 4.0)
    return (signal + noise_part).astype(jnp.bfloat16)


def place_ends(values, stream_key, low, largest):
    shape = values.shape
    spot = [jax.random.randint(jax.random.fold_in(stream_key, axis), (), 0, shape[axis]) for axis in range(len(shape))]
    values = values.at[tuple(spot)].set(low)
    longest = shape.index(max(shape))
    spot[longest] = (spot[longest] + 1) % shape[longest]
    return values.at[tuple(spot)].set(largest)


def levels(own_key, shape, cuts, least, top_value):
    def one(position, blocks):
        heights = jax.random.uniform(jax.random.fold_in(jax.random.fold_in(own_key, 6), position), (blocks,), jnp.float32, least / len(cuts), top_value / len(cuts))
        return jnp.repeat(jnp.exp(heights), shape[position] // blocks).reshape((-1,) + (1,) * (len(shape) - position - 1))

    loudness = one(*cuts[0])
    for cut in cuts[1:]:
        loudness = loudness * one(*cut)
    return loudness


def routed_block(own_key, own, number, rows, count, top, bound, lean):
    sequence = jax.random.permutation(own_key, count)
    packed, ordinary = load_shares(count, rows * top, bound, lean, True), load_shares(count, rows * top, bound, lean, False)
    places = jnp.arange(count)

    def named(tallies, offset_by):
        used = int((tallies > 0).sum())
        fixed = max(1, used // 4)
        passed = fixed + (places - fixed + offset_by * (used - fixed)) % max(1, count - fixed)
        return jnp.zeros((count,), jnp.int32).at[sequence[jnp.where(places < fixed, places, passed)]].set(jnp.asarray(tallies, jnp.int32))

    tallies = jnp.where(number % 4 == 0, named(packed, number // 4), named(ordinary, number - number // 4 - 1))
    mixed = jax.random.permutation(jax.random.fold_in(own, 3), count)
    giver, sink = mixed[0:count // 2 * 2:2], mixed[1:count // 2 * 2:2]
    slack = jnp.minimum(tallies[giver] - 1, bound - tallies[sink]) // 2
    slack = jnp.where((giver == sequence[0]) | (sink == sequence[0]) | (tallies[sink] == 0), 0, jnp.maximum(slack, 0))
    passed = jax.random.randint(jax.random.fold_in(own, 4), (count // 2,), 0, 1 << 20) % (slack + 1)
    tallies = tallies.at[giver].add(-passed).at[sink].add(passed)
    members = jnp.searchsorted(jnp.cumsum(tallies), jnp.arange(rows * top), side="right").astype(jnp.int32)
    grid = members.reshape(top, rows).T
    grid = grid[jax.random.permutation(jax.random.fold_in(own, 1), rows)]
    offset_by = jax.random.randint(jax.random.fold_in(own, 2), (rows, 1), 0, top)
    return jnp.take_along_axis(grid, (jnp.arange(top)[None, :] + offset_by) % top, axis=1)


def load_shares(count, total, reach, skew, full):
    portions = [(1 << 20) // math.isqrt(grade ** skew) + 1 for grade in range(1, count + 1)]
    largest = reach if full else min(reach, max(-(-total // count), total * portions[0] // sum(portions)))
    least = 1 if total - largest >= count - 1 else 0
    given, spare = [largest] + [least] * (count - 1), total - largest - least * (count - 1)
    while spare > 0:
        free = [i for i in range(1, count) if given[i] < largest] or [i for i in range(1, count) if given[i] < reach]
        pool, budget = sum([portions[i] for i in free]), spare
        for i in free:
            more = min(reach - given[i], max(1, budget * portions[i] // pool), spare)
            given[i] = given[i] + more
            spare = spare - more
    return np.array(given)


def setup_inputs(seed: int = 0, part: int = 0) -> dict:
    key_of = jax.random.split(jax.random.key(seed), 8)
    part_splits = jax.random.split(jax.random.fold_in(key_of[7], part), 8)
    particles = draw_particles(jax.random.fold_in(jax.random.fold_in(key_of[7], part), 71), part)
    ctf_index = place_ends(jax.random.randint(part_splits[1], (PTOT,), 0, NCTF), jax.random.fold_in(part_splits[1], 1), 0, NCTF - 1).astype(jnp.int32)
    beta = jnp.clip(jnp.exp(math.log(60.0) - 1.7917595 * jax.random.uniform(part_splits[2], (PTOT,), jnp.float32) ** levels(part_splits[2], (PTOT,), ((0, 16),), -0.2, 0.2)), 10.0, 60.0).astype(jnp.bfloat16)
    significant_keys = jax.random.split(jax.random.fold_in(part_splits[3], 1), NBLK // NB)
    significant_turns = jax.random.permutation(jax.random.fold_in(part_splits[3], 3), NBLK // NB)
    significant = jax.vmap(lambda own, number: routed_block(jax.random.fold_in(part_splits[3], 2), own, number, NB, NGRP, SIG, CAP, 3))(significant_keys, significant_turns).reshape((NBLK, SIG))
    ctf_table = jnp.clip(jax.random.uniform(key_of[4], (NCTF, NPIX), jnp.float32, 0.049804688, 1.0), 0.049804688, 1.0).astype(jnp.bfloat16)
    references = draw_references(jax.random.fold_in(jax.random.fold_in(key_of[7], part), 71), part)
    offsets = draw_offsets(jax.random.fold_in(jax.random.fold_in(key_of[7], part), 71), part)
    return {"particles": particles, "ctf_index": ctf_index, "beta": beta, "significant": significant, "ctf_table": ctf_table, "references": references, "offsets": offsets}


EPSILON = 1e-06

def phase_tables(offsets):
    pixel_index = jnp.arange(KX * KY, dtype=jnp.int32)
    freq_x = pixel_index % KX
    freq_y = pixel_index // KX - KY // 2
    phase_rotations = jnp.mod(offsets[:, 0:1] * freq_x[None, :] + offsets[:, 1:2] * freq_y[None, :], BOX)
    angles = phase_rotations.astype(jnp.float32) * (2.0 * math.pi / BOX)
    return (jnp.cos(angles), jnp.sin(angles))

def shifted_table(refs_now, cosines, sines):
    real_part = refs_now[:, 0, :].astype(jnp.float32)
    imag_part = refs_now[:, 1, :].astype(jnp.float32)
    translation_real = real_part[None] * cosines[:, None] + imag_part[None] * sines[:, None]
    shift_imag = imag_part[None] * cosines[:, None] - real_part[None] * sines[:, None]
    shifted = jnp.stack([translation_real, shift_imag], axis=2).astype(jnp.bfloat16)
    return shifted.reshape(shifted.shape[0] * shifted.shape[1], 2 * shifted.shape[3])

def ref_energy(refs_now):
    return lax.optimization_barrier(jnp.sum(jnp.square(refs_now.astype(jnp.float32)), axis=1))

def reference(particles, ctf_index, beta, significant, ctf_table, references, offsets):
    cosines, sines = phase_tables(offsets)
    ctf_rows = jnp.take(ctf_table, ctf_index, axis=0)
    particle_images = particles.astype(jnp.float32)
    weighted = (ctf_rows.astype(jnp.float32)[:, None, :] * particle_images).astype(jnp.bfloat16).reshape(PTOT, 2 * NPIX)
    image_power = lax.optimization_barrier(jnp.sum(particle_images * particle_images, axis=(1, 2)))
    ctf_squares = jnp.square(ctf_rows.astype(jnp.float32))
    inverse_noise = beta.astype(jnp.float32)
    block_of = jnp.arange(PTOT, dtype=jnp.int32) // BLK
    listed = jnp.any(significant[:, :, None] == jnp.arange(NGRP, dtype=jnp.int32)[None, None, :], axis=1).astype(jnp.float32)
    member_entry = jnp.take(listed, block_of, axis=0)

    def per_group(group_id):

        def per_class(class_id):
            refs_now = references[class_id, group_id]
            shifted = shifted_table(refs_now, cosines, sines)
            intersection = lax.dot_general(weighted, shifted, (((1,), (1,)), ((), ())), preferred_element_type=jnp.float32)
            energy = ref_energy(refs_now)
            ref_power = lax.dot_general(ctf_squares, energy, (((1,), (1,)), ((), ())), precision=lax.Precision.HIGHEST, preferred_element_type=jnp.float32)
            intersection = intersection.reshape(PTOT, T_OFF, OR_G)
            normalizer = jnp.sqrt(image_power[:, None] * ref_power + EPSILON)
            logits = inverse_noise[:, None, None] * intersection / normalizer[:, None, :]
            return lax.optimization_barrier(jnp.sum(jnp.exp(logits), axis=(1, 2)))
        return lax.map(per_class, jnp.arange(NCLS, dtype=jnp.int32))
    grouped_rows = lax.map(per_group, jnp.arange(NGRP, dtype=jnp.int32))
    marginal_evidence = jnp.einsum('ysm,my->ms', grouped_rows, member_entry, precision=lax.Precision.HIGHEST)
    all_classes = lax.optimization_barrier(jnp.sum(marginal_evidence, axis=1))
    return (marginal_evidence / all_classes[:, None], jnp.log(all_classes))
```

```python
import functools
import math

import jax
import jax.numpy as jnp
from jax import lax
from jax.experimental import pallas as pl
from jax.experimental.pallas import tpu as pltpu
from jax.sharding import PartitionSpec as P

BOX = 256
KX = 129
KY = 128
EPSILON = 1e-06
LANES = 128
MESH = pl.DeviceIdType.MESH
HIGHEST = lax.Precision.HIGHEST
NT = (((1,), (1,)), ((), ()))


def repeat(count, body):
    if count <= 8:
        for step in range(count):
            body(step)
    else:
        pl.loop(0, count)(body)


def sine(quarter):
    x = quarter * (math.pi / 128)
    s = x * x
    p = -2.5052108e-08
    p = p * s + 2.7557319e-06
    p = p * s - 1.9841270e-04
    p = p * s + 8.3333333e-03
    p = p * s - 1.6666667e-01
    return x + x * (s * p)


def kernel(
    zs, xs, blocks, listed, shifts, codes, rows, pixels, wide,
    index_ref, sig_ref, off_ref, beta_ref, part_hbm, table_hbm, refs_hbm,
    post_ref, log_ref,
    land, part, table, ctf, shifted, rsq, csq, tp, acc, power,
    in_sem, land_sem, sib_sem, tp_sem, zsend, xsend, sibsend, tpsend,
):
    z, x, h = lax.axis_index("orient"), lax.axis_index("cls"), lax.axis_index("dom")
    peers = zs * xs
    me = x * zs + z
    half = wide // 2
    tiles = pixels // LANES
    mine = pl.ds(pl.multiple_of(h * half, LANES), half)
    theirs = pl.ds(pl.multiple_of((1 - h) * half, LANES), half)
    barrier = pltpu.get_barrier_semaphore()

    def peer(offset):
        number = lax.rem(me + offset, peers)
        return {"orient": lax.rem(number, zs), "cls": lax.div(number, zs)}

    @functools.partial(repeat, peers - 1)
    def _(i):
        pl.semaphore_signal(barrier, inc=1, device_id=peer(i + 1), device_id_type=MESH)

    pl.semaphore_signal(barrier, inc=1, device_id={"dom": 1 - h}, device_id_type=MESH)
    loads = [
        pltpu.make_async_copy(part_hbm, part, in_sem.at[0]),
        pltpu.make_async_copy(table_hbm, table, in_sem.at[1]),
        pltpu.make_async_copy(refs_hbm, land.at[x, z], in_sem.at[2]),
    ]
    for load in loads:
        load.start()
    pl.semaphore_wait(barrier, peers)

    def z_copy(zz, direction, src):
        return pltpu.make_async_remote_copy(
            src_ref=src, dst_ref=land.at[x, zz, :, mine],
            send_sem=zsend.at[direction, zz], recv_sem=land_sem.at[x, zz],
            device_id={"orient": z + 1 - 2 * direction}, device_id_type=MESH,
        )

    def x_copy(c, zz, direction, src):
        return pltpu.make_async_remote_copy(
            src_ref=src, dst_ref=land.at[c, zz, :, mine],
            send_sem=xsend.at[direction, c, zz], recv_sem=land_sem.at[c, zz],
            device_id={"cls": x + 1 - 2 * direction}, device_id_type=MESH,
        )

    def sib_copy(c, zz):
        return pltpu.make_async_remote_copy(
            src_ref=land.at[c, zz, :, mine], dst_ref=land.at[c, zz, :, mine],
            send_sem=sibsend.at[c, zz], recv_sem=sib_sem.at[c, zz],
            device_id={"dom": 1 - h}, device_id_type=MESH,
        )

    def z_targets(zz):
        return (z < zs - 1) & (zz <= z), (z > 0) & (zz >= z)

    def x_targets(c):
        return (x < xs - 1) & (c <= x), (x > 0) & (c >= x)

    own = refs_hbm.at[:, mine]
    for direction, wanted in enumerate(z_targets(z)):
        pl.when(wanted)(lambda d=direction: z_copy(z, d, own).start())
    for direction, wanted in enumerate(x_targets(x)):
        pl.when(wanted)(lambda d=direction: x_copy(x, z, d, own).start())

    def landed(c, zz):
        pltpu.make_async_copy(land.at[c, zz, :, mine], land.at[c, zz, :, mine], land_sem.at[c, zz]).wait()

    def from_z(zz):
        landed(x, zz)
        src = land.at[x, zz, :, mine]
        for direction, wanted in enumerate(z_targets(zz)):
            pl.when(wanted)(lambda d=direction: z_copy(zz, d, src).start())
        for direction, wanted in enumerate(x_targets(x)):
            pl.when(wanted)(lambda d=direction: x_copy(x, zz, d, src).start())
        sib_copy(x, zz).start()

    def z_step(step):
        for zz in (z - step - 1, z + step + 1):
            pl.when((zz >= 0) & (zz < zs))(lambda zz=zz: from_z(zz))

    def from_x(c, zz):
        landed(c, zz)
        src = land.at[c, zz, :, mine]
        for direction, wanted in enumerate(x_targets(c)):
            pl.when(wanted)(lambda d=direction: x_copy(c, zz, d, src).start())
        sib_copy(c, zz).start()

    def x_step(step, zstep):
        for c in (x - step - 1, x + step + 1):
            for zz in (z - zstep, z + zstep) if not (isinstance(zstep, int) and zstep == 0) else (z,):
                pl.when((c >= 0) & (c < xs) & (zz >= 0) & (zz < zs))(lambda c=c, zz=zz: from_x(c, zz))

    row = lax.broadcasted_iota(jnp.int32, (rows, 1), 0)
    lane = lax.broadcasted_iota(jnp.int32, (1, LANES), 1)

    code_of = jnp.zeros((rows, codes), jnp.int32)
    row_codes = lax.broadcasted_iota(jnp.int32, (rows, codes), 0) // 2
    for p in range(rows // 2):
        code_of = jnp.where(row_codes == p, index_ref[p], code_of)
    choice = (code_of == lax.broadcasted_iota(jnp.int32, (rows, codes), 1)).astype(jnp.float32)

    for load in loads:
        load.wait()

    @pl.loop(0, tiles)
    def _(k):
        at = pl.ds(pl.multiple_of(k * LANES, LANES), LANES)
        r = land[x, z, :, at].astype(jnp.float32)
        r = r * r
        high = r.astype(jnp.bfloat16).astype(jnp.float32)
        rsq[:, at] = jnp.concatenate([high, r - high], axis=0).astype(jnp.bfloat16)
        c = table[:, at].astype(jnp.float32)
        c = c * c
        high = c.astype(jnp.bfloat16).astype(jnp.float32)
        csq[:, at] = jnp.concatenate([high, c - high], axis=0).astype(jnp.bfloat16)

    products = lax.dot_general(csq[...], rsq[...], NT, preferred_element_type=jnp.float32)
    products = products[:codes] + products[codes:]
    eight = land.shape[2]
    products = products[:, :eight] + products[:, eight:]
    spread = jnp.concatenate([products, jnp.zeros((codes, LANES - eight), jnp.float32)], axis=1)
    tp[x, z] = pltpu.roll(spread, z * eight, 1)

    def tp_copy(offset):
        return pltpu.make_async_remote_copy(
            src_ref=tp.at[x, z], dst_ref=tp.at[x, z],
            send_sem=tpsend.at[offset], recv_sem=tp_sem.at[x, z],
            device_id=peer(offset), device_id_type=MESH,
        )

    repeat(peers - 1, lambda i: tp_copy(i + 1).start())

    ctf[...] = jnp.dot(
        choice.astype(jnp.bfloat16), table[...], preferred_element_type=jnp.float32
    ).astype(jnp.bfloat16)
    z_step(0)

    trow = lax.broadcasted_iota(jnp.int32, (8, LANES), 0)
    tx = jnp.zeros((8, LANES), jnp.int32)
    ty = jnp.zeros((8, LANES), jnp.int32)
    for t in range(shifts):
        tx = jnp.where(trow == t, off_ref[t, 0], tx)
        ty = jnp.where(trow == t, off_ref[t, 1], ty)
    lanes8 = lax.broadcasted_iota(jnp.int32, (8, LANES), 1)
    odd = (lax.broadcasted_iota(jnp.int32, (rows, LANES), 0) % 2) == 1
    power[...] = jnp.zeros_like(power)
    if wide > pixels:
        shifted[:, pl.ds(pixels, wide - pixels)] = jnp.zeros((shifts * rows, wide - pixels), jnp.bfloat16)

    def turn(k):
        at = pl.ds(pl.multiple_of(k * LANES, LANES), LANES)
        j = lanes8 + k * LANES
        line = ((j.astype(jnp.float32) + 0.5) * (1.0 / KX)).astype(jnp.int32)
        m = (tx * (j - line * KX) + ty * (line - KY // 2)) & (BOX - 1)
        m = m.astype(jnp.float32)
        fold = BOX // 4 - jnp.abs(m - BOX // 2)
        sines = sine(jnp.where(m < BOX // 2, 1.0, -1.0) * (BOX // 4 - jnp.abs(BOX // 4 - jnp.where(m < BOX // 2, m, m - BOX // 2))))
        cosines = -sine(fold)
        image = part[:, at].astype(jnp.float32)
        power[...] += image * image
        w = (image * ctf[:, at].astype(jnp.float32)).astype(jnp.bfloat16).astype(jnp.float32)
        other = jnp.where(odd, pltpu.roll(w, 1, 0), -pltpu.roll(w, rows - 1, 0))
        for t in range(shifts):
            turned = w * cosines[t:t + 1] + other * sines[t:t + 1]
            shifted[pl.ds(t * rows, rows), at] = turned.astype(jnp.bfloat16)

    stages = 3
    cuts = [tiles * i // stages for i in range(stages + 1)]

    def turns(stage):
        pl.loop(cuts[stage], cuts[stage + 1])(turn)

    turns(0)
    repeat_from = functools.partial(x_step, 0)
    repeat_from(0)
    if zs > 2:
        z_step(1)
    turns(1)
    repeat_from(1)
    turns(2)
    if zs > 3:
        z_step(2)
    if zs > 4:
        pl.loop(3, zs - 1)(z_step)
    if zs > 2:
        pl.loop(2, zs)(repeat_from)
    for step in range(1, xs - 1):
        x_step(step, 0)
        pl.loop(1, zs)(functools.partial(x_step, step))

    def everyone(i):
        c, zz = lax.div(i, zs), lax.rem(i, zs)

        @pl.when(i != me)
        def _():
            dst = land.at[c, zz, :, theirs]
            pltpu.make_async_copy(dst, dst, sib_sem.at[c, zz]).wait()
            pltpu.make_async_copy(tp.at[c, zz], tp.at[c, zz], tp_sem.at[c, zz]).wait()

    repeat(peers, everyone)

    image_power = jnp.sum(power[...], axis=1, keepdims=True)
    image_power = image_power + jnp.where(row % 2 == 1, pltpu.roll(jnp.broadcast_to(image_power, (rows, LANES)), 1, 0), pltpu.roll(jnp.broadcast_to(image_power, (rows, LANES)), rows - 1, 0))
    beta_lane = lax.broadcasted_iota(jnp.int32, (rows, rows // 2), 1)
    beta_row = lax.broadcasted_iota(jnp.int32, (rows, rows // 2), 0) // 2
    beta = jnp.sum(jnp.where(beta_lane == beta_row, beta_ref[...].astype(jnp.float32), 0.0), axis=1, keepdims=True)
    member = jnp.zeros((rows, LANES), jnp.bool_)
    group = lax.broadcasted_iota(jnp.int32, (rows, LANES), 1) // eight
    block = lax.broadcasted_iota(jnp.int32, (rows, LANES), 0) // (rows // blocks)
    for b in range(blocks):
        for s in range(listed):
            member = member | ((block == b) & (group == sig_ref[b, s]))
    lane_all = lax.broadcasted_iota(jnp.int32, (rows, LANES), 1)
    member = member & (lane_all % 2 == 0) & (lane_all < zs * eight)
    step_k = wide
    for parts in (5, 13):
        if step_k % (parts * 256) == 0 and step_k > 3328:
            step_k = wide // parts
    acc[...] = jnp.zeros_like(acc)
    evidence = jnp.zeros((rows, LANES), jnp.float32)
    for c in range(xs):
        def dots(i, total):
            at = pl.ds(pl.multiple_of(i * step_k, LANES), step_k)
            refs = land[c, :, :, at].reshape(zs * eight, step_k)
            return total + lax.dot_general(shifted[:, at], refs, NT, preferred_element_type=jnp.float32)

        total = lax.fori_loop(0, wide // step_k, dots, jnp.zeros((shifts * rows, zs * eight), jnp.float32))
        acc[:, pl.ds(0, zs * eight)] = total
        both = acc[...]
        arow = lax.broadcasted_iota(jnp.int32, both.shape, 0)
        acol = lax.broadcasted_iota(jnp.int32, both.shape, 1)
        both = jnp.where(arow % 2 == acol % 2, both, 0.0)
        both = both + pltpu.roll(both, shifts * rows - 1, 0)
        both = both + pltpu.roll(both, LANES - 1, 1)
        table_power = tp[c, 0]
        for zz in range(1, zs):
            table_power = table_power + tp[c, zz]
        ref_power = jnp.dot(choice, table_power, precision=HIGHEST, preferred_element_type=jnp.float32)
        ref_power = ref_power + pltpu.roll(ref_power, LANES - 1, 1)
        scale = beta / jnp.sqrt(image_power * ref_power + EPSILON)
        summed = jnp.zeros((rows, LANES), jnp.float32)
        for t in range(shifts):
            summed = summed + jnp.exp(both[t * rows:(t + 1) * rows] * scale)
        found = jnp.sum(jnp.where(member, summed, 0.0), axis=1, keepdims=True)
        evidence = jnp.where(lane_all == c, found, evidence)

    half_rows = rows // 2
    pick = (
        lax.broadcasted_iota(jnp.int32, (half_rows, rows), 1)
        == 2 * lax.broadcasted_iota(jnp.int32, (half_rows, rows), 0)
    ).astype(jnp.float32)
    evidence = jnp.dot(pick, jnp.where(odd, 0.0, evidence), precision=HIGHEST, preferred_element_type=jnp.float32)
    total = jnp.sum(evidence, axis=1, keepdims=True)
    post_ref[...] = (evidence / total)[:, :xs]
    diagonal = lax.broadcasted_iota(jnp.int32, (half_rows, half_rows), 0) == lax.broadcasted_iota(
        jnp.int32, (half_rows, half_rows), 1
    )
    log_ref[...] = jnp.sum(jnp.where(diagonal, jnp.log(total), 0.0), axis=0, keepdims=True)

    def sent(i):
        c, zz = lax.div(i, zs), lax.rem(i, zs)
        pl.when(i != me)(lambda: sib_copy(c, zz).wait_send())

        @pl.when(c == x)
        def _():
            for direction, wanted in enumerate(z_targets(zz)):
                pl.when(wanted)(lambda d=direction: z_copy(zz, d, own).wait_send())

        for direction, wanted in enumerate(x_targets(c)):
            pl.when(wanted)(lambda d=direction: x_copy(c, zz, d, own).wait_send())

    repeat(peers, sent)
    repeat(peers - 1, lambda i: tp_copy(i + 1).wait_send())


def local(particles, ctf_index, beta, significant, ctf_table, references, offsets):
    zs, xs = lax.axis_size("orient"), lax.axis_size("cls")
    count, _, pixels = particles.shape
    orients = references.shape[2]
    eight, rows = 2 * orients, 2 * count
    codes = ctf_table.shape[0]
    shifts = offsets.shape[0]
    wide = -(-pixels // 256) * 256
    refs = jnp.pad(references.reshape(eight, pixels), ((0, 0), (0, wide - pixels)))
    parts = particles.reshape(rows, pixels)
    smem = pl.BlockSpec(memory_space=pltpu.SMEM)
    vmem = pl.BlockSpec(memory_space=pltpu.VMEM)
    anywhere = pl.BlockSpec(memory_space=pl.ANY)
    dma = pltpu.SemaphoreType.DMA
    post, logs = pl.pallas_call(
        functools.partial(
            kernel, zs, xs, significant.shape[0], significant.shape[1], shifts, codes, rows, pixels, wide
        ),
        out_shape=(
            jax.ShapeDtypeStruct((count, xs), jnp.float32),
            jax.ShapeDtypeStruct((1, count), jnp.float32),
        ),
        in_specs=[smem, smem, smem, vmem, anywhere, anywhere, anywhere],
        out_specs=(vmem, vmem),
        scratch_shapes=[
            pltpu.VMEM((xs, zs, eight, wide), jnp.bfloat16),
            pltpu.VMEM((rows, pixels), jnp.bfloat16),
            pltpu.VMEM((codes, pixels), jnp.bfloat16),
            pltpu.VMEM((rows, pixels), jnp.bfloat16),
            pltpu.VMEM((shifts * rows, wide), jnp.bfloat16),
            pltpu.VMEM((2 * eight, pixels), jnp.bfloat16),
            pltpu.VMEM((2 * codes, pixels), jnp.bfloat16),
            pltpu.VMEM((xs, zs, codes, LANES), jnp.float32),
            pltpu.VMEM((shifts * rows, LANES), jnp.float32),
            pltpu.VMEM((rows, LANES), jnp.float32),
            dma((3,)),
            dma((xs, zs)),
            dma((xs, zs)),
            dma((xs, zs)),
            dma((2, zs)),
            dma((2, xs, zs)),
            dma((xs, zs)),
            dma((xs * zs,)),
        ],
        compiler_params=pltpu.CompilerParams(
            collective_id=0, has_side_effects=True, vmem_limit_bytes=58 * 2**20
        ),
    )(ctf_index, significant, offsets, beta.reshape(1, count), parts, ctf_table, refs)
    return post, logs.reshape(count)


def solution(mesh):
    everyone = ("groups", "orient", "cls", "dom")
    return jax.shard_map(
        local,
        mesh=mesh,
        in_specs=(
            P(everyone, None, None),
            P(everyone),
            P(everyone),
            P(everyone, None),
            P(),
            P(("groups", "cls"), "orient", None, None, None),
            P("groups", None),
        ),
        out_specs=(P(everyone, None), P(everyone)),
        check_vma=False,
    )
```

```python
import functools
import math

import jax
import jax.numpy as jnp
from jax import lax
from jax.experimental import pallas as pl
from jax.experimental.pallas import tpu as pltpu
from jax.sharding import PartitionSpec as P

BOX = 256
KX = 129
KY = 128
EPSILON = 1e-06
LANES = 128
MESH = pl.DeviceIdType.MESH
HIGHEST = lax.Precision.HIGHEST
NT = (((1,), (1,)), ((), ()))


def repeat(count, body):
    if count <= 8:
        for step in range(count):
            body(step)
    else:
        pl.loop(0, count)(body)


def sine(quarter):
    x = quarter * (math.pi / 128)
    s = x * x
    p = -2.5052108e-08
    p = p * s + 2.7557319e-06
    p = p * s - 1.9841270e-04
    p = p * s + 8.3333333e-03
    p = p * s - 1.6666667e-01
    return x + x * (s * p)


def kernel(
    zs, xs, blocks, listed, shifts, codes, rows, pixels,
    index_ref, sig_ref, off_ref, beta_ref, part_hbm, table_hbm, refs_hbm,
    out_ref,
    part3, land, table, ctf, shifted, rsq, csq, tp, acc, power,
    in_sem, land_sem, sib_sem, tp_sem, zsend, xsend, sibsend, tpsend,
):
    z, x, h = lax.axis_index("orient"), lax.axis_index("cls"), lax.axis_index("dom")
    peers = zs * xs
    eight = 2 * land.shape[2]
    me = x * zs + z
    half = land.shape[2] // 2
    tiles = pixels // LANES
    mine = pl.ds(h * half, half)
    theirs = pl.ds((1 - h) * half, half)
    barrier = pltpu.get_barrier_semaphore()

    def peer(offset):
        number = lax.rem(me + offset, peers)
        return {"orient": lax.rem(number, zs), "cls": lax.div(number, zs)}

    @functools.partial(repeat, peers - 1)
    def _(i):
        pl.semaphore_signal(barrier, inc=1, device_id=peer(i + 1), device_id_type=MESH)

    pl.semaphore_signal(barrier, inc=1, device_id={"dom": 1 - h}, device_id_type=MESH)
    loads = [
        pltpu.make_async_copy(part_hbm, part3, in_sem.at[0]),
        pltpu.make_async_copy(table_hbm, table, in_sem.at[1]),
        pltpu.make_async_copy(refs_hbm, land.at[x, z], in_sem.at[2]),
    ]
    for load in loads:
        load.start()
    pl.semaphore_wait(barrier, peers)

    def z_copy(zz, direction, src):
        return pltpu.make_async_remote_copy(
            src_ref=src, dst_ref=land.at[x, zz, mine],
            send_sem=zsend.at[direction, zz], recv_sem=land_sem.at[x, zz],
            device_id={"orient": z + 1 - 2 * direction}, device_id_type=MESH,
        )

    def x_copy(c, zz, direction, src):
        return pltpu.make_async_remote_copy(
            src_ref=src, dst_ref=land.at[c, zz, mine],
            send_sem=xsend.at[direction, c, zz], recv_sem=land_sem.at[c, zz],
            device_id={"cls": x + 1 - 2 * direction}, device_id_type=MESH,
        )

    def sib_copy(c, zz):
        return pltpu.make_async_remote_copy(
            src_ref=land.at[c, zz, mine], dst_ref=land.at[c, zz, mine],
            send_sem=sibsend.at[c, zz], recv_sem=sib_sem.at[c, zz],
            device_id={"dom": 1 - h}, device_id_type=MESH,
        )

    def z_targets(zz):
        return (z < zs - 1) & (zz <= z), (z > 0) & (zz >= z)

    def x_targets(c):
        return (x < xs - 1) & (c <= x), (x > 0) & (c >= x)

    own = refs_hbm.at[mine]
    for direction, wanted in enumerate(z_targets(z)):
        pl.when(wanted)(lambda d=direction: z_copy(z, d, own).start())
    for direction, wanted in enumerate(x_targets(x)):
        pl.when(wanted)(lambda d=direction: x_copy(x, z, d, own).start())

    def landed(c, zz):
        pltpu.make_async_copy(land.at[c, zz, mine], land.at[c, zz, mine], land_sem.at[c, zz]).wait()

    def from_z(zz):
        landed(x, zz)
        src = land.at[x, zz, mine]
        for direction, wanted in enumerate(z_targets(zz)):
            pl.when(wanted)(lambda d=direction: z_copy(zz, d, src).start())
        for direction, wanted in enumerate(x_targets(x)):
            pl.when(wanted)(lambda d=direction: x_copy(x, zz, d, src).start())
        sib_copy(x, zz).start()

    def z_step(step):
        for zz in (z - step - 1, z + step + 1):
            pl.when((zz >= 0) & (zz < zs))(lambda zz=zz: from_z(zz))

    def from_x(c, zz):
        landed(c, zz)
        src = land.at[c, zz, mine]
        for direction, wanted in enumerate(x_targets(c)):
            pl.when(wanted)(lambda d=direction: x_copy(c, zz, d, src).start())
        sib_copy(c, zz).start()

    def x_step(step, zstep):
        for c in (x - step - 1, x + step + 1):
            for zz in (z - zstep, z + zstep) if not (isinstance(zstep, int) and zstep == 0) else (z,):
                pl.when((c >= 0) & (c < xs) & (zz >= 0) & (zz < zs))(lambda c=c, zz=zz: from_x(c, zz))

    row = lax.broadcasted_iota(jnp.int32, (rows, 1), 0)
    lane = lax.broadcasted_iota(jnp.int32, (1, LANES), 1)

    code_of = jnp.zeros((rows, codes), jnp.int32)
    row_codes = lax.broadcasted_iota(jnp.int32, (rows, codes), 0) // 2
    for p in range(rows // 2):
        code_of = jnp.where(row_codes == p, index_ref[p], code_of)
    choice = (code_of == lax.broadcasted_iota(jnp.int32, (rows, codes), 1)).astype(jnp.float32)

    for load in loads:
        load.wait()

    @pl.loop(0, tiles)
    def _(k):
        at = pl.ds(pl.multiple_of(k * LANES, LANES), LANES)
        r = land[x, z, :, :, at].reshape(eight, LANES).astype(jnp.float32)
        r = r * r
        high = r.astype(jnp.bfloat16).astype(jnp.float32)
        rsq[:, at] = jnp.concatenate([high, r - high], axis=0).astype(jnp.bfloat16)
        c = table[:, at].astype(jnp.float32)
        c = c * c
        high = c.astype(jnp.bfloat16).astype(jnp.float32)
        csq[:, at] = jnp.concatenate([high, c - high], axis=0).astype(jnp.bfloat16)

    products = lax.dot_general(csq[...], rsq[...], NT, preferred_element_type=jnp.float32)
    products = products[:codes] + products[codes:]
    products = products[:, :eight] + products[:, eight:]
    spread = jnp.concatenate([products, jnp.zeros((codes, LANES - eight), jnp.float32)], axis=1)
    tp[x, z] = pltpu.roll(spread, z * eight, 1)

    def tp_copy(offset):
        return pltpu.make_async_remote_copy(
            src_ref=tp.at[x, z], dst_ref=tp.at[x, z],
            send_sem=tpsend.at[offset], recv_sem=tp_sem.at[x, z],
            device_id=peer(offset), device_id_type=MESH,
        )

    repeat(peers - 1, lambda i: tp_copy(i + 1).start())

    ctf[...] = jnp.dot(
        choice.astype(jnp.bfloat16), table[...], preferred_element_type=jnp.float32
    ).astype(jnp.bfloat16)
    z_step(0)

    trow = lax.broadcasted_iota(jnp.int32, (8, LANES), 0)
    tx = jnp.zeros((8, LANES), jnp.int32)
    ty = jnp.zeros((8, LANES), jnp.int32)
    for t in range(shifts):
        tx = jnp.where(trow == t, off_ref[0, t], tx)
        ty = jnp.where(trow == t, off_ref[1, t], ty)
    lanes8 = lax.broadcasted_iota(jnp.int32, (8, LANES), 1)
    odd = (lax.broadcasted_iota(jnp.int32, (rows, LANES), 0) % 2) == 1
    power[...] = jnp.zeros_like(power)

    def turn(k):
        at = pl.ds(pl.multiple_of(k * LANES, LANES), LANES)
        j = lanes8 + k * LANES
        line = ((j.astype(jnp.float32) + 0.5) * (1.0 / KX)).astype(jnp.int32)
        m = (tx * (j - line * KX) + ty * (line - KY // 2)) & (BOX - 1)
        m = m.astype(jnp.float32)
        fold = BOX // 4 - jnp.abs(m - BOX // 2)
        sines = sine(jnp.where(m < BOX // 2, 1.0, -1.0) * (BOX // 4 - jnp.abs(BOX // 4 - jnp.where(m < BOX // 2, m, m - BOX // 2))))
        cosines = -sine(fold)
        image = part3[:, :, at].reshape(rows, LANES).astype(jnp.float32)
        power[...] += image * image
        w = (image * ctf[:, at].astype(jnp.float32)).astype(jnp.bfloat16).astype(jnp.float32)
        other = jnp.where(odd, pltpu.roll(w, 1, 0), -pltpu.roll(w, rows - 1, 0))
        for t in range(shifts):
            turned = w * cosines[t:t + 1] + other * sines[t:t + 1]
            shifted[pl.ds(t * rows, rows), at] = turned.astype(jnp.bfloat16)

    stages = 3
    cuts = [tiles * i // stages for i in range(stages + 1)]

    def turns(stage):
        pl.loop(cuts[stage], cuts[stage + 1])(turn)

    turns(0)
    repeat_from = functools.partial(x_step, 0)
    repeat_from(0)
    if zs > 2:
        z_step(1)
    turns(1)
    repeat_from(1)
    turns(2)
    if zs > 3:
        z_step(2)
    if zs > 4:
        pl.loop(3, zs - 1)(z_step)
    if zs > 3:
        pl.loop(2, zs - 1)(repeat_from)

    def complete(c, zz):

        @pl.when((c != x) | (zz != z))
        def _():
            dst = land.at[c, zz, theirs]
            pltpu.make_async_copy(dst, dst, sib_sem.at[c, zz]).wait()
            pltpu.make_async_copy(tp.at[c, zz], tp.at[c, zz], tp_sem.at[c, zz]).wait()

    image_power = jnp.sum(power[...], axis=1, keepdims=True)
    image_power = image_power + jnp.where(row % 2 == 1, pltpu.roll(jnp.broadcast_to(image_power, (rows, LANES)), 1, 0), pltpu.roll(jnp.broadcast_to(image_power, (rows, LANES)), rows - 1, 0))
    beta_lane = lax.broadcasted_iota(jnp.int32, (rows, rows // 2), 1)
    beta_row = lax.broadcasted_iota(jnp.int32, (rows, rows // 2), 0) // 2
    beta = jnp.sum(jnp.where(beta_lane == beta_row, beta_ref[...].astype(jnp.float32), 0.0), axis=1, keepdims=True)
    member = jnp.zeros((rows, LANES), jnp.bool_)
    group = lax.broadcasted_iota(jnp.int32, (rows, LANES), 1) // eight
    block = lax.broadcasted_iota(jnp.int32, (rows, LANES), 0) // (rows // blocks)
    for b in range(blocks):
        for s in range(listed):
            member = member | ((block == b) & (group == sig_ref[b * listed + s]))
    lane_all = lax.broadcasted_iota(jnp.int32, (rows, LANES), 1)
    member = member & (lane_all % 2 == 0) & (lane_all < zs * eight)
    acc[...] = jnp.zeros_like(acc)
    step_k = next(pixels // n for n in (3, 5, 1) if tiles % n == 0)

    def score(c, evidence):
        def dots(i, total):
            at = pl.ds(pl.multiple_of(i * step_k, LANES), step_k)
            refs = land[c, :, :, :, at].reshape(zs * eight, step_k)
            return total + lax.dot_general(shifted[:, at], refs, NT, preferred_element_type=jnp.float32)

        total = lax.fori_loop(0, pixels // step_k, dots, jnp.zeros((shifts * rows, zs * eight), jnp.float32))
        acc[:, pl.ds(0, zs * eight)] = total
        both = acc[...]
        arow = lax.broadcasted_iota(jnp.int32, both.shape, 0)
        acol = lax.broadcasted_iota(jnp.int32, both.shape, 1)
        both = jnp.where(arow % 2 == acol % 2, both, 0.0)
        both = both + pltpu.roll(both, shifts * rows - 1, 0)
        both = both + pltpu.roll(both, LANES - 1, 1)
        table_power = tp[c, 0]
        for zz in range(1, zs):
            table_power = table_power + tp[c, zz]
        ref_power = jnp.dot(choice, table_power, precision=HIGHEST, preferred_element_type=jnp.float32)
        ref_power = ref_power + pltpu.roll(ref_power, LANES - 1, 1)
        scale = beta / jnp.sqrt(image_power * ref_power + EPSILON)
        summed = jnp.zeros((rows, LANES), jnp.float32)
        for t in range(shifts):
            summed = summed + jnp.exp(both[t * rows:(t + 1) * rows] * scale)
        found = jnp.sum(jnp.where(member, summed, 0.0), axis=1, keepdims=True)
        return jnp.where(lane_all == c, found, evidence)

    repeat(zs, lambda zz: complete(x, zz))
    evidence = score(x, jnp.zeros((rows, LANES), jnp.float32))
    if zs > 2:
        repeat_from(zs - 1)
    for step in range(1, xs - 1):
        x_step(step, 0)
        pl.loop(1, zs)(functools.partial(x_step, step))
    for i in range(1, xs):
        c = lax.rem(x + i, xs)
        repeat(zs, functools.partial(complete, c))
        evidence = score(c, evidence)

    half_rows = rows // 2
    pick = (
        lax.broadcasted_iota(jnp.int32, (half_rows, rows), 1)
        == 2 * lax.broadcasted_iota(jnp.int32, (half_rows, rows), 0)
    ).astype(jnp.float32)
    evidence = jnp.dot(pick, jnp.where(odd, 0.0, evidence), precision=HIGHEST, preferred_element_type=jnp.float32)
    diagonal = lax.broadcasted_iota(jnp.int32, (half_rows, half_rows), 0) == lax.broadcasted_iota(
        jnp.int32, (half_rows, half_rows), 1
    )
    for c in range(xs):
        out_ref[c:c + 1, :] = jnp.sum(jnp.where(diagonal, evidence[:, c:c + 1], 0.0), axis=0, keepdims=True)

    def sent(i):
        c, zz = lax.div(i, zs), lax.rem(i, zs)
        pl.when(i != me)(lambda: sib_copy(c, zz).wait_send())

        @pl.when(c == x)
        def _():
            for direction, wanted in enumerate(z_targets(zz)):
                pl.when(wanted)(lambda d=direction: z_copy(zz, d, own).wait_send())

        for direction, wanted in enumerate(x_targets(c)):
            pl.when(wanted)(lambda d=direction: x_copy(c, zz, d, own).wait_send())

    repeat(peers, sent)
    repeat(peers - 1, lambda i: tp_copy(i + 1).wait_send())


def local(particles, ctf_index, beta, significant, ctf_table, references, offsets):
    zs, xs = lax.axis_size("orient"), lax.axis_size("cls")
    count, _, pixels = particles.shape
    orients = references.shape[2]
    eight, rows = 2 * orients, 2 * count
    codes = ctf_table.shape[0]
    shifts = offsets.shape[0]
    refs = references.reshape(orients, 2, pixels)
    parts = particles
    smem = pl.BlockSpec(memory_space=pltpu.SMEM)
    vmem = pl.BlockSpec(memory_space=pltpu.VMEM)
    anywhere = pl.BlockSpec(memory_space=pl.ANY)
    dma = pltpu.SemaphoreType.DMA
    evidence = pl.pallas_call(
        functools.partial(
            kernel, zs, xs, significant.shape[0], significant.shape[1], shifts, codes, rows, pixels
        ),
        out_shape=jax.ShapeDtypeStruct((xs, count), jnp.float32),
        in_specs=[smem, smem, smem, vmem, anywhere, anywhere, anywhere],
        out_specs=vmem,
        scratch_shapes=[
            pltpu.VMEM((count, 2, pixels), jnp.bfloat16),
            pltpu.VMEM((xs, zs, orients, 2, pixels), jnp.bfloat16),
            pltpu.VMEM((codes, pixels), jnp.bfloat16),
            pltpu.VMEM((rows, pixels), jnp.bfloat16),
            pltpu.VMEM((shifts * rows, pixels), jnp.bfloat16),
            pltpu.VMEM((2 * eight, pixels), jnp.bfloat16),
            pltpu.VMEM((2 * codes, pixels), jnp.bfloat16),
            pltpu.VMEM((xs, zs, codes, LANES), jnp.float32),
            pltpu.VMEM((shifts * rows, LANES), jnp.float32),
            pltpu.VMEM((rows, LANES), jnp.float32),
            dma((3,)),
            dma((xs, zs)),
            dma((xs, zs)),
            dma((xs, zs)),
            dma((2, zs)),
            dma((2, xs, zs)),
            dma((xs, zs)),
            dma((xs * zs,)),
        ],
        compiler_params=pltpu.CompilerParams(
            collective_id=0, has_side_effects=True, vmem_limit_bytes=58 * 2**20
        ),
    )(ctf_index, significant.reshape(-1), offsets.T, beta.reshape(1, count), parts, ctf_table, refs)
    total = jnp.sum(evidence, axis=0)
    return (evidence / total[None]).T, jnp.log(total)


def solution(mesh):
    everyone = ("groups", "orient", "cls", "dom")
    return jax.shard_map(
        local,
        mesh=mesh,
        in_specs=(
            P(everyone, None, None),
            P(everyone),
            P(everyone),
            P(everyone, None),
            P(),
            P(("groups", "cls"), "orient", None, None, None),
            P("groups", None),
        ),
        out_specs=(P(everyone, None), P(everyone)),
        check_vma=False,
    )
```

```python
import functools
import math

import jax
import jax.numpy as jnp
from jax import lax
from jax.experimental import pallas as pl
from jax.experimental.pallas import tpu as pltpu
from jax.sharding import PartitionSpec as P

BOX = 256
KX = 129
KY = 128
EPSILON = 1e-06
LANES = 128
MESH = pl.DeviceIdType.MESH
HIGHEST = lax.Precision.HIGHEST
NT = (((1,), (1,)), ((), ()))


def repeat(count, body):
    if count <= 8:
        for step in range(count):
            body(step)
    else:
        pl.loop(0, count)(body)


def sine(quarter):
    x = quarter * (math.pi / 128)
    s = x * x
    p = -2.5052108e-08
    p = p * s + 2.7557319e-06
    p = p * s - 1.9841270e-04
    p = p * s + 8.3333333e-03
    p = p * s - 1.6666667e-01
    return x + x * (s * p)


def kernel(
    zs, xs, blocks, listed, shifts, codes, rows, pixels,
    index_ref, sig_ref, off_ref, beta_ref, part_hbm, table_hbm, refs_hbm,
    out_ref,
    part3, land, table, ctf, shifted, rsq, csq, tp, acc, power,
    in_sem, land_sem, sib_sem, tp_sem, zsend, xsend, sibsend, tpsend,
):
    z, x, h = lax.axis_index("orient"), lax.axis_index("cls"), lax.axis_index("dom")
    peers = zs * xs
    eight = 2 * land.shape[2]
    me = x * zs + z
    half = land.shape[2] // 2
    tiles = pixels // LANES
    mine = pl.ds(h * half, half)
    theirs = pl.ds((1 - h) * half, half)
    barrier = pltpu.get_barrier_semaphore()

    def peer(offset):
        number = lax.rem(me + offset, peers)
        return {"orient": lax.rem(number, zs), "cls": lax.div(number, zs)}

    @functools.partial(repeat, peers - 1)
    def _(i):
        pl.semaphore_signal(barrier, inc=1, device_id=peer(i + 1), device_id_type=MESH)

    pl.semaphore_signal(barrier, inc=1, device_id={"dom": 1 - h}, device_id_type=MESH)
    loads = [
        pltpu.make_async_copy(part_hbm, part3, in_sem.at[0]),
        pltpu.make_async_copy(table_hbm, table, in_sem.at[1]),
        pltpu.make_async_copy(refs_hbm, land.at[x, z], in_sem.at[2]),
    ]
    for load in loads:
        load.start()
    pl.semaphore_wait(barrier, peers)

    def z_copy(zz, direction, src):
        return pltpu.make_async_remote_copy(
            src_ref=src, dst_ref=land.at[x, zz, mine],
            send_sem=zsend.at[direction, zz], recv_sem=land_sem.at[x, zz],
            device_id={"orient": z + 1 - 2 * direction}, device_id_type=MESH,
        )

    def x_copy(c, zz, direction, src):
        return pltpu.make_async_remote_copy(
            src_ref=src, dst_ref=land.at[c, zz, mine],
            send_sem=xsend.at[direction, c, zz], recv_sem=land_sem.at[c, zz],
            device_id={"cls": x + 1 - 2 * direction}, device_id_type=MESH,
        )

    def sib_copy(c, zz):
        return pltpu.make_async_remote_copy(
            src_ref=land.at[c, zz, mine], dst_ref=land.at[c, zz, mine],
            send_sem=sibsend.at[c, zz], recv_sem=sib_sem.at[c, zz],
            device_id={"dom": 1 - h}, device_id_type=MESH,
        )

    def z_targets(zz):
        return (z < zs - 1) & (zz <= z), (z > 0) & (zz >= z)

    def x_targets(c):
        return (x < xs - 1) & (c <= x), (x > 0) & (c >= x)

    own = refs_hbm.at[mine]
    for direction, wanted in enumerate(z_targets(z)):
        pl.when(wanted)(lambda d=direction: z_copy(z, d, own).start())
    for direction, wanted in enumerate(x_targets(x)):
        pl.when(wanted)(lambda d=direction: x_copy(x, z, d, own).start())

    def landed(c, zz):
        pltpu.make_async_copy(land.at[c, zz, mine], land.at[c, zz, mine], land_sem.at[c, zz]).wait()

    def from_z(zz):
        landed(x, zz)
        src = land.at[x, zz, mine]
        for direction, wanted in enumerate(z_targets(zz)):
            pl.when(wanted)(lambda d=direction: z_copy(zz, d, src).start())
        for direction, wanted in enumerate(x_targets(x)):
            pl.when(wanted)(lambda d=direction: x_copy(x, zz, d, src).start())
        sib_copy(x, zz).start()

    def z_step(step):
        for zz in (z - step - 1, z + step + 1):
            pl.when((zz >= 0) & (zz < zs))(lambda zz=zz: from_z(zz))

    def from_x(c, zz):
        landed(c, zz)
        src = land.at[c, zz, mine]
        for direction, wanted in enumerate(x_targets(c)):
            pl.when(wanted)(lambda d=direction: x_copy(c, zz, d, src).start())
        sib_copy(c, zz).start()

    def x_step(step, zstep):
        for c in (x - step - 1, x + step + 1):
            for zz in (z - zstep, z + zstep) if not (isinstance(zstep, int) and zstep == 0) else (z,):
                pl.when((c >= 0) & (c < xs) & (zz >= 0) & (zz < zs))(lambda c=c, zz=zz: from_x(c, zz))

    row = lax.broadcasted_iota(jnp.int32, (rows, 1), 0)
    lane = lax.broadcasted_iota(jnp.int32, (1, LANES), 1)

    code_of = jnp.zeros((rows, codes), jnp.int32)
    row_codes = lax.broadcasted_iota(jnp.int32, (rows, codes), 0) // 2
    for p in range(rows // 2):
        code_of = jnp.where(row_codes == p, index_ref[p], code_of)
    choice = (code_of == lax.broadcasted_iota(jnp.int32, (rows, codes), 1)).astype(jnp.float32)

    for load in loads:
        load.wait()

    @pl.loop(0, tiles, unroll=3)
    def _(k):
        at = pl.ds(pl.multiple_of(k * LANES, LANES), LANES)
        r = land[x, z, :, :, at].reshape(eight, LANES).astype(jnp.float32)
        r = r * r
        high = r.astype(jnp.bfloat16).astype(jnp.float32)
        rsq[:, at] = jnp.concatenate([high, r - high], axis=0).astype(jnp.bfloat16)
        c = table[:, at].astype(jnp.float32)
        c = c * c
        high = c.astype(jnp.bfloat16).astype(jnp.float32)
        csq[:, at] = jnp.concatenate([high, c - high], axis=0).astype(jnp.bfloat16)

    products = lax.dot_general(csq[...], rsq[...], NT, preferred_element_type=jnp.float32)
    products = products[:codes] + products[codes:]
    products = products[:, :eight] + products[:, eight:]
    spread = jnp.concatenate([products, jnp.zeros((codes, LANES - eight), jnp.float32)], axis=1)
    tp[x, z] = pltpu.roll(spread, z * eight, 1)

    def tp_copy(offset):
        return pltpu.make_async_remote_copy(
            src_ref=tp.at[x, z], dst_ref=tp.at[x, z],
            send_sem=tpsend.at[offset], recv_sem=tp_sem.at[x, z],
            device_id=peer(offset), device_id_type=MESH,
        )

    repeat(peers - 1, lambda i: tp_copy(i + 1).start())

    ctf[...] = jnp.dot(
        choice.astype(jnp.bfloat16), table[...], preferred_element_type=jnp.float32
    ).astype(jnp.bfloat16)
    z_step(0)

    trow = lax.broadcasted_iota(jnp.int32, (8, LANES), 0)
    tx = jnp.zeros((8, LANES), jnp.int32)
    ty = jnp.zeros((8, LANES), jnp.int32)
    for t in range(shifts):
        tx = jnp.where(trow == t, off_ref[0, t], tx)
        ty = jnp.where(trow == t, off_ref[1, t], ty)
    lanes8 = lax.broadcasted_iota(jnp.int32, (8, LANES), 1)
    odd = (lax.broadcasted_iota(jnp.int32, (rows, LANES), 0) % 2) == 1
    power[...] = jnp.zeros_like(power)

    def turn(k):
        at = pl.ds(pl.multiple_of(k * LANES, LANES), LANES)
        j = lanes8 + k * LANES
        line = ((j.astype(jnp.float32) + 0.5) * (1.0 / KX)).astype(jnp.int32)
        m = (tx * (j - line * KX) + ty * (line - KY // 2)) & (BOX - 1)
        m = m.astype(jnp.float32)
        fold = BOX // 4 - jnp.abs(m - BOX // 2)
        sines = sine(jnp.where(m < BOX // 2, 1.0, -1.0) * (BOX // 4 - jnp.abs(BOX // 4 - jnp.where(m < BOX // 2, m, m - BOX // 2))))
        cosines = -sine(fold)
        image = part3[:, :, at].reshape(rows, LANES).astype(jnp.float32)
        power[...] += image * image
        w = (image * ctf[:, at].astype(jnp.float32)).astype(jnp.bfloat16).astype(jnp.float32)
        other = jnp.where(odd, pltpu.roll(w, 1, 0), -pltpu.roll(w, rows - 1, 0))
        for t in range(shifts):
            turned = w * cosines[t:t + 1] + other * sines[t:t + 1]
            shifted[pl.ds(t * rows, rows), at] = turned.astype(jnp.bfloat16)

    stages = 3
    cuts = [tiles * i // stages for i in range(stages + 1)]

    def turns(stage):
        pl.loop(cuts[stage], cuts[stage + 1], unroll=2)(turn)

    turns(0)
    repeat_from = functools.partial(x_step, 0)
    repeat_from(0)
    if zs > 2:
        z_step(1)
    turns(1)
    repeat_from(1)
    turns(2)
    if zs > 3:
        z_step(2)
    if zs > 4:
        pl.loop(3, zs - 1)(z_step)
    if zs > 3:
        pl.loop(2, zs - 1)(repeat_from)

    def complete(c, zz):

        @pl.when((c != x) | (zz != z))
        def _():
            dst = land.at[c, zz, theirs]
            pltpu.make_async_copy(dst, dst, sib_sem.at[c, zz]).wait()
            pltpu.make_async_copy(tp.at[c, zz], tp.at[c, zz], tp_sem.at[c, zz]).wait()

    image_power = jnp.sum(power[...], axis=1, keepdims=True)
    image_power = image_power + jnp.where(row % 2 == 1, pltpu.roll(jnp.broadcast_to(image_power, (rows, LANES)), 1, 0), pltpu.roll(jnp.broadcast_to(image_power, (rows, LANES)), rows - 1, 0))
    beta_lane = lax.broadcasted_iota(jnp.int32, (rows, rows // 2), 1)
    beta_row = lax.broadcasted_iota(jnp.int32, (rows, rows // 2), 0) // 2
    beta = jnp.sum(jnp.where(beta_lane == beta_row, beta_ref[...].astype(jnp.float32), 0.0), axis=1, keepdims=True)
    member = jnp.zeros((rows, LANES), jnp.bool_)
    group = lax.broadcasted_iota(jnp.int32, (rows, LANES), 1) // eight
    block = lax.broadcasted_iota(jnp.int32, (rows, LANES), 0) // (rows // blocks)
    for b in range(blocks):
        for s in range(listed):
            member = member | ((block == b) & (group == sig_ref[b * listed + s]))
    lane_all = lax.broadcasted_iota(jnp.int32, (rows, LANES), 1)
    member = member & (lane_all % 2 == 0) & (lane_all < zs * eight)
    acc[...] = jnp.zeros_like(acc)
    step_k = next(pixels // n for n in (3, 5, 1) if tiles % n == 0)

    def score(c, evidence):
        def dots(i, total):
            at = pl.ds(pl.multiple_of(i * step_k, LANES), step_k)
            refs = land[c, :, :, :, at].reshape(zs * eight, step_k)
            return total + lax.dot_general(shifted[:, at], refs, NT, preferred_element_type=jnp.float32)

        total = lax.fori_loop(0, pixels // step_k, dots, jnp.zeros((shifts * rows, zs * eight), jnp.float32))
        acc[:, pl.ds(0, zs * eight)] = total
        both = acc[...]
        arow = lax.broadcasted_iota(jnp.int32, both.shape, 0)
        acol = lax.broadcasted_iota(jnp.int32, both.shape, 1)
        both = jnp.where(arow % 2 == acol % 2, both, 0.0)
        both = both + pltpu.roll(both, shifts * rows - 1, 0)
        both = both + pltpu.roll(both, LANES - 1, 1)
        table_power = tp[c, 0]
        for zz in range(1, zs):
            table_power = table_power + tp[c, zz]
        ref_power = jnp.dot(choice, table_power, precision=HIGHEST, preferred_element_type=jnp.float32)
        ref_power = ref_power + pltpu.roll(ref_power, LANES - 1, 1)
        scale = beta / jnp.sqrt(image_power * ref_power + EPSILON)
        summed = jnp.zeros((rows, LANES), jnp.float32)
        for t in range(shifts):
            summed = summed + jnp.exp(both[t * rows:(t + 1) * rows] * scale)
        found = jnp.sum(jnp.where(member, summed, 0.0), axis=1, keepdims=True)
        return jnp.where(lane_all == c, found, evidence)

    repeat(zs, lambda zz: complete(x, zz))
    evidence = score(x, jnp.zeros((rows, LANES), jnp.float32))
    if zs > 2:
        repeat_from(zs - 1)
    for step in range(1, xs - 1):
        x_step(step, 0)
        pl.loop(1, zs)(functools.partial(x_step, step))
    for i in range(1, xs):
        c = lax.rem(x + i, xs)
        repeat(zs, functools.partial(complete, c))
        evidence = score(c, evidence)

    half_rows = rows // 2
    pick = (
        lax.broadcasted_iota(jnp.int32, (half_rows, rows), 1)
        == 2 * lax.broadcasted_iota(jnp.int32, (half_rows, rows), 0)
    ).astype(jnp.float32)
    evidence = jnp.dot(pick, jnp.where(odd, 0.0, evidence), precision=HIGHEST, preferred_element_type=jnp.float32)
    diagonal = lax.broadcasted_iota(jnp.int32, (half_rows, half_rows), 0) == lax.broadcasted_iota(
        jnp.int32, (half_rows, half_rows), 1
    )
    for c in range(xs):
        out_ref[c:c + 1, :] = jnp.sum(jnp.where(diagonal, evidence[:, c:c + 1], 0.0), axis=0, keepdims=True)

    def sent(i):
        c, zz = lax.div(i, zs), lax.rem(i, zs)
        pl.when(i != me)(lambda: sib_copy(c, zz).wait_send())

        @pl.when(c == x)
        def _():
            for direction, wanted in enumerate(z_targets(zz)):
                pl.when(wanted)(lambda d=direction: z_copy(zz, d, own).wait_send())

        for direction, wanted in enumerate(x_targets(c)):
            pl.when(wanted)(lambda d=direction: x_copy(c, zz, d, own).wait_send())

    repeat(peers, sent)
    repeat(peers - 1, lambda i: tp_copy(i + 1).wait_send())


def local(particles, ctf_index, beta, significant, ctf_table, references, offsets):
    zs, xs = lax.axis_size("orient"), lax.axis_size("cls")
    count, _, pixels = particles.shape
    orients = references.shape[2]
    eight, rows = 2 * orients, 2 * count
    codes = ctf_table.shape[0]
    shifts = offsets.shape[0]
    refs = references.reshape(orients, 2, pixels)
    parts = particles
    smem = pl.BlockSpec(memory_space=pltpu.SMEM)
    vmem = pl.BlockSpec(memory_space=pltpu.VMEM)
    anywhere = pl.BlockSpec(memory_space=pl.ANY)
    dma = pltpu.SemaphoreType.DMA
    evidence = pl.pallas_call(
        functools.partial(
            kernel, zs, xs, significant.shape[0], significant.shape[1], shifts, codes, rows, pixels
        ),
        out_shape=jax.ShapeDtypeStruct((xs, count), jnp.float32),
        in_specs=[smem, smem, smem, vmem, anywhere, anywhere, anywhere],
        out_specs=vmem,
        scratch_shapes=[
            pltpu.VMEM((count, 2, pixels), jnp.bfloat16),
            pltpu.VMEM((xs, zs, orients, 2, pixels), jnp.bfloat16),
            pltpu.VMEM((codes, pixels), jnp.bfloat16),
            pltpu.VMEM((rows, pixels), jnp.bfloat16),
            pltpu.VMEM((shifts * rows, pixels), jnp.bfloat16),
            pltpu.VMEM((2 * eight, pixels), jnp.bfloat16),
            pltpu.VMEM((2 * codes, pixels), jnp.bfloat16),
            pltpu.VMEM((xs, zs, codes, LANES), jnp.float32),
            pltpu.VMEM((shifts * rows, LANES), jnp.float32),
            pltpu.VMEM((rows, LANES), jnp.float32),
            dma((3,)),
            dma((xs, zs)),
            dma((xs, zs)),
            dma((xs, zs)),
            dma((2, zs)),
            dma((2, xs, zs)),
            dma((xs, zs)),
            dma((xs * zs,)),
        ],
        compiler_params=pltpu.CompilerParams(
            collective_id=0, has_side_effects=True, vmem_limit_bytes=58 * 2**20
        ),
    )(ctf_index, significant.reshape(-1), offsets.T, beta.reshape(1, count), parts, ctf_table, refs)
    total = jnp.sum(evidence, axis=0)
    return (evidence / total[None]).T, jnp.log(total)


def solution(mesh):
    everyone = ("groups", "orient", "cls", "dom")
    return jax.shard_map(
        local,
        mesh=mesh,
        in_specs=(
            P(everyone, None, None),
            P(everyone),
            P(everyone),
            P(everyone, None),
            P(),
            P(("groups", "cls"), "orient", None, None, None),
            P("groups", None),
        ),
        out_specs=(P(everyone, None), P(everyone)),
        check_vma=False,
    )
```
